256 devices in a mesh: dp: 2 (over core), seq: 128 (over z, x, y).
Axes of the slice: x: 4, y: 4, z: 8, core: 2. Of those that a mesh axis runs over, the one named last changes fastest.
Arguments:
- signal: bfloat16 [2, 16384, 512], P('dp', 'seq'), may hold values from -6 to 6
- grad_out: bfloat16 [2, 16384, 512], P('dp', 'seq'), may hold values from -6 to 6
- mode_coef: float32 [2, 2, 64, 512], replicated, may hold values from -6 to 6
- decay_param: float32 [2, 64, 512], replicated, may hold values from 0.1 to 370
- freq_index: int32 [2, 64, 512], replicated, may hold values from 0 to 4095
- skip_gain: float32 [512], replicated, may hold values from -4 to 4
Outputs:
- grad_signal: bfloat16 [2, 16384, 512], P('dp', 'seq')
- grad_coef: float32 [2, 2, 64, 512], replicated
- grad_skip: float32 [512], replicated
The draws below stay inside these ranges and needn't reach their ends.
All inputs are finite; a program needn't handle non-finite values.
Results may differ from the reference program's by a relative error of at most 0.011.
Values may be sent and summed in bfloat16 or wider, within the bound.
A program may use at most 64 MiB of HBM per device.

```python
import math
import jax
import jax.numpy as jnp
from jax import lax

CHANNELS = 512
MODES = 64
SEQ_LEN = 16384
SEQS = 2


def shared_source(key):
    return jax.random.truncated_normal(key, -6.0, 6.0, (SEQS, SEQ_LEN, CHANNELS), jnp.float32)


def draw_signal(key, part):
    source = shared_source(key)
    return source.astype(jnp.bfloat16)


def draw_grad_out(key, part):
    source = shared_source(key)
    key = jax.random.fold_in(key, 11)
    jitter = jax.random.truncated_normal(key, -6.0, 6.0, (SEQS, SEQ_LEN, CHANNELS), jnp.float32)
    offset = SEQ_LEN // 64
    delayed = jnp.pad(source, ((0, 0), (offset, 0), (0, 0)))[:, :SEQ_LEN]
    advanced = jnp.pad(source, ((0, 0), (0, offset), (0, 0)))[:, offset:]
    blended = jnp.clip(0.5 * delayed + 0.5 * advanced + 0.7 * jitter, -6.0, 6.0)
    return blended.astype(jnp.bfloat16)


def draw_decay_param(key, part):
    key = jax.random.fold_in(key, 5)
    chooser_key, lasting_key, fleeting_key = jax.random.split(key, 3)
    extent = (2, MODES, CHANNELS)
    chooser = jax.random.uniform(chooser_key, extent, jnp.float32)
    lasting = jnp.exp(jax.random.uniform(lasting_key, extent, jnp.float32, minval=math.log(0.1), maxval=math.log(4.0)))
    fleeting = jax.random.uniform(fleeting_key, extent, jnp.float32, minval=250.0, maxval=370.0)
    return jnp.where(chooser < 0.25, lasting, fleeting).astype(jnp.float32)


def set_ends(result, stream_key, least, top_value):
    longest = result.shape.index(max(result.shape))
    spots = []
    for shift in (0, 1):
        where = [jax.random.randint(jax.random.fold_in(stream_key, axis), (), 0, length) for axis, length in enumerate(result.shape)]
        where[longest] = (where[longest] + shift) % result.shape[longest]
        spots.append(tuple(where))
    return result.at[spots[0]].set(least).at[spots[1]].set(top_value)


def noise(key, dims, deviation, bound, kind=jnp.bfloat16):
    return jnp.clip(deviation * jax.random.normal(key, dims, jnp.float32), -bound, bound).astype(kind)


def setup_inputs(seed: int = 0) -> dict:
    streams_of = jax.random.split(jax.random.key(seed), 7)
    return {
        "signal": draw_signal(jax.random.fold_in(streams_of[6], 71), 0),
        "grad_out": draw_grad_out(jax.random.fold_in(streams_of[6], 71), 0),
        "mode_coef": noise(streams_of[2], (2, 2, MODES, CHANNELS), 1.0, 6.0, jnp.float32),
        "decay_param": draw_decay_param(jax.random.fold_in(streams_of[6], 71), 0),
        "freq_index": set_ends(jax.random.randint(streams_of[4], (2, MODES, CHANNELS), 0, SEQ_LEN // 4), jax.random.fold_in(streams_of[4], 1), 0, (SEQ_LEN // 4) - 1).astype(jnp.int32),
        "skip_gain": noise(streams_of[5], (CHANNELS,), 1.0, 4.0, jnp.float32),
    }


def exact_turns(freq_index, lag_list, period):
    lag_high = lag_list // 1024
    lag_low = lag_list % 1024
    return (((freq_index * lag_high) % period) * 1024 + freq_index * lag_low) % period


def fade_wave(decay_rate, freq_index, lag_list):
    turns = exact_turns(freq_index[None, :], lag_list[:, None], SEQ_LEN)
    angle = turns.astype(jnp.float32) * (2.0 * math.pi / SEQ_LEN)
    fade_out = jnp.exp(-decay_rate[None, :] * lag_list[:, None].astype(jnp.float32))
    return fade_out * jnp.cos(angle), fade_out * jnp.sin(angle)


def kernel_half(coef_dir, rate_dir, freq_dir, lag_list, kernel_scale):
    def mode_step(running, mode_slice):
        coef_re, coef_im, decay_rate, freq_index = mode_slice
        wave_cos, wave_sin = fade_wave(decay_rate, freq_index, lag_list)
        return running + (coef_re[None, :] * wave_cos - coef_im[None, :] * wave_sin), None

    start_zero = jnp.zeros((lag_list.shape[0], CHANNELS), jnp.float32)
    running, _ = lax.scan(mode_step, start_zero, (coef_dir[0], coef_dir[1], rate_dir, freq_dir))
    return 2.0 * kernel_scale * running


def coef_grad_half(weights, rate_dir, freq_dir, lag_list, kernel_scale):
    def mode_step(carry, mode_slice):
        decay_rate, freq_index = mode_slice
        wave_cos, wave_sin = fade_wave(decay_rate, freq_index, lag_list)
        return carry, jnp.stack([jnp.sum(weights * wave_cos, axis=0), -jnp.sum(weights * wave_sin, axis=0)])

    _, rows_out = lax.scan(mode_step, jnp.zeros((), jnp.float32), (rate_dir, freq_dir))
    return 2.0 * kernel_scale * jnp.swapaxes(rows_out, 0, 1)


def reference(signal, grad_out, mode_coef, decay_param, freq_index, skip_gain):
    kernel_scale = (MODES * SEQ_LEN) ** -0.5
    decay_rate = decay_param / SEQ_LEN
    lag_list = jnp.arange(SEQ_LEN, dtype=jnp.int32)
    kernel_fwd = kernel_half(mode_coef[0], decay_rate[0], freq_index[0], lag_list, kernel_scale)
    kernel_bwd = kernel_half(mode_coef[1], decay_rate[1], freq_index[1], lag_list, kernel_scale)
    upper_half = jnp.concatenate([jnp.zeros((1, CHANNELS), jnp.float32), kernel_bwd[1:][::-1]], axis=0)
    kernel_spec = jnp.fft.fft(jnp.concatenate([kernel_fwd, upper_half], axis=0), axis=0)
    padding = jnp.zeros((SEQ_LEN, CHANNELS), jnp.float32)
    kernel_grad = jnp.zeros((2 * SEQ_LEN, CHANNELS), jnp.float32)
    grad_skip = jnp.zeros((CHANNELS,), jnp.float32)
    outputs = []
    for seq_id in range(SEQS):
        seq_signal = signal[seq_id].astype(jnp.float32)
        seq_cotan = grad_out[seq_id].astype(jnp.float32)
        signal_spec = jnp.fft.fft(jnp.concatenate([seq_signal, padding], axis=0), axis=0)
        cotan_spec = jnp.fft.fft(jnp.concatenate([seq_cotan, padding], axis=0), axis=0)
        through = jnp.real(jnp.fft.ifft(cotan_spec * jnp.conj(kernel_spec), axis=0))[:SEQ_LEN]
        outputs.append((through + skip_gain[None, :] * seq_cotan).astype(jnp.bfloat16))
        kernel_grad = kernel_grad + jnp.real(jnp.fft.ifft(cotan_spec * jnp.conj(signal_spec), axis=0))
        grad_skip = grad_skip + jnp.sum(seq_cotan * seq_signal, axis=0)
    weights_bwd = jnp.concatenate([jnp.zeros((1, CHANNELS), jnp.float32), kernel_grad[SEQ_LEN + 1:][::-1]], axis=0)
    grad_coef = jnp.stack([
        coef_grad_half(kernel_grad[:SEQ_LEN], decay_rate[0], freq_index[0], lag_list, kernel_scale),
        coef_grad_half(weights_bwd, decay_rate[1], freq_index[1], lag_list, kernel_scale)])
    return jnp.stack(outputs), grad_coef, grad_skip
```

```python
import math

import jax
import jax.numpy as jnp
import numpy as np
from jax import lax
from jax.sharding import PartitionSpec as P

highest = lax.Precision.HIGHEST
AXES = ("dp", "seq")


def tables(blocks, width):
    half = blocks
    period = 2 * blocks * width
    odd = 2 * np.arange(half) + 1
    angle = 2.0 * np.pi * (odd[:, None] * np.arange(2 * blocks)[None, :] % (4 * blocks)) / (4 * blocks)
    sign = np.where(np.arange(2 * blocks) < blocks, 1.0, -1.0)[None, :]
    outer = np.concatenate([np.cos(angle) * sign, -np.sin(angle) * sign], axis=0)
    angle = 2.0 * np.pi * (odd[:, None] * np.arange(width)[None, :]) / (2 * period)
    twist_cos, twist_sin = np.cos(angle), np.sin(angle)
    angle = 2.0 * np.pi * (np.arange(width)[:, None] * np.arange(width)[None, :] % width) / width
    cos, sin = np.cos(angle), np.sin(angle)
    inner = np.block([[cos, -sin], [sin, cos]])
    back = np.block([[cos, sin], [-sin, cos]])
    return [np.asarray(t, np.float32) for t in (outer, twist_cos, twist_sin, inner, back)]


def cos_turns(turns, length):
    quarter = length // 4
    v = (jnp.abs(turns - length // 2) - quarter).astype(jnp.float32) * (1.0 / quarter)
    w = v * v
    poly = 0.00015148419
    for c in (-0.00467376557, 0.07968967928, -0.64596371106, 1.57079631847):
        poly = poly * w + c
    return poly * v


def fade_table(rate, freq, lag, length, modes):
    lane = lax.broadcasted_iota(jnp.int32, (1, 2 * modes), 1)
    shift = jnp.where(lane < modes, 0, length - length // 4)
    turns = (freq * lag + shift) % length
    return jnp.exp(-rate * lag.astype(jnp.float32)) * cos_turns(turns, length)


def local_part(sig, cot, coef, rate, freq, skip, blocks, width):
    outer, twist_cos, twist_sin, inner, back = tables(blocks, width)
    channels, seqs = sig.shape[:2]
    length = blocks * width
    modes = rate.shape[1]
    scale = 2.0 * (modes * length) ** (-0.5)
    einsum = lambda *a: jnp.einsum(*a, precision=highest)

    def forward(x, table):
        a = einsum("ks,gsp->gkp", table, x)
        re, im = a[:, :blocks], a[:, blocks:]
        both = jnp.concatenate([re * twist_cos + im * twist_sin, im * twist_cos - re * twist_sin], axis=2)
        s = einsum("gkp,pq->gkq", both, inner)
        return s[:, :, :width], s[:, :, width:]

    def inverse(re, im, table):
        b = einsum("gkq,qp->gkp", jnp.concatenate([re, im], axis=2), back)
        re, im = b[:, :, :width], b[:, :, width:]
        both = jnp.concatenate([re * twist_cos - im * twist_sin, im * twist_cos + re * twist_sin], axis=1)
        return einsum("ks,gkp->gsp", table, both) * (1.0 / length)

    low = lax.broadcasted_iota(jnp.int32, (blocks, 1), 0)
    inn = lax.broadcasted_iota(jnp.int32, (width, 1), 0)
    lags = ((low * width, inn), ((blocks - 1 - low) * width, width - inn))
    live = jnp.where((low == 0) & (inn.T == 0), 0.0, 1.0)
    kern, fades = [], []
    for c in range(channels):
        halves = []
        for d in range(2):
            rate2 = jnp.tile(rate[d, :, c], 2)[None]
            freq2 = jnp.tile(freq[d, :, c], 2)[None]
            fa = fade_table(rate2, freq2, lags[d][0], length, modes)
            fb = fade_table(rate2, freq2, lags[d][1], length, modes)
            cre, cim = coef[d, 0, :, c], coef[d, 1, :, c]
            c1 = jnp.concatenate([cre, -cre])[None]
            c2 = jnp.concatenate([-cim, -cim])[None]
            mixed = c1 * fa + c2 * jnp.roll(fa, modes, axis=1)
            half = einsum("sn,pn->sp", mixed, fb) * scale
            halves.append(half if d == 0 else half * live)
            fades.append((fa, fb))
        kern.append(jnp.concatenate(halves, axis=0))
    kre, kim = forward(jnp.stack(kern), outer)
    flat = lambda t: t.reshape((channels * seqs, blocks, width)).astype(jnp.float32)
    sre, sim = forward(flat(sig), outer[:, :blocks])
    gre, gim = forward(flat(cot), outer[:, :blocks])
    kre, kim = (jnp.repeat(t, seqs, axis=0) for t in (kre, kim))
    out = inverse(gre * kre + gim * kim, gim * kre - gre * kim, outer[:, :blocks])
    corr = lambda t: t.reshape((channels, seqs, blocks, width)).sum(axis=1)
    wts = inverse(corr(gre * sre + gim * sim), corr(gim * sre - gre * sim), outer)
    out = out.reshape(cot.shape) + skip[:, None, None, None] * cot.astype(jnp.float32)
    rows = []
    for c in range(channels):
        for d in range(2):
            fa, fb = fades[c * 2 + d]
            w = wts[c, d * blocks:(d + 1) * blocks]
            if d:
                w = w * live
            t = einsum("sp,pn->sn", w, fb)
            p = jnp.sum(fa * t, axis=0)
            q = jnp.sum(fa * jnp.roll(t, modes, axis=1), axis=0)
            rows.append(jnp.concatenate([p[:modes] - p[modes:], -(q[:modes] + q[modes:])]) * scale)
    grads = jnp.stack(rows).reshape(channels, 2, 2, modes)
    skips = jnp.sum(flat(sig) * flat(cot), axis=(1, 2)).reshape(channels, seqs).sum(axis=1)
    return out.astype(jnp.bfloat16), grads, skips


def on_device(signal, grad_out, mode_coef, decay_param, freq_index, skip_gain):
    seq_count = lax.axis_size("seq")
    devices = lax.axis_size("dp") * seq_count
    width, channels = signal.shape[1:]
    each = channels // devices
    length = width * seq_count
    seqs = lax.axis_size("dp")
    mine = lax.axis_index(AXES) * each
    both = jnp.stack([signal[0], grad_out[0]]).transpose(2, 0, 1).reshape(devices, each, 2, width)
    got = lax.all_to_all(both, AXES, split_axis=0, concat_axis=0, tiled=True)
    got = got.reshape(seqs, seq_count, each, 2, width).transpose(3, 2, 0, 1, 4)
    take = lambda t: lax.dynamic_slice_in_dim(t, mine, each, t.ndim - 1)
    out, grads, skips = local_part(
        got[0], got[1], take(mode_coef), take(decay_param) / float(length), take(freq_index), take(skip_gain),
        seq_count, width)
    back = out.transpose(1, 2, 0, 3).reshape(devices, each, width)
    back = lax.all_to_all(back, AXES, split_axis=0, concat_axis=0, tiled=True)
    grad_signal = back.reshape(channels, width).T[None]
    flat = jnp.concatenate([grads.reshape(each, -1), skips[:, None]], axis=1)
    flat = lax.all_gather(flat, AXES, axis=0, tiled=True)
    grad_coef = flat[:, :-1].T.reshape(mode_coef.shape)
    return (grad_signal, grad_coef, flat[:, -1])


def solution(mesh):
    return jax.shard_map(
        on_device,
        mesh=mesh,
        in_specs=(P("dp", "seq", None), P("dp", "seq", None), P(), P(), P(), P()),
        out_specs=(P("dp", "seq", None), P(), P()),
        check_vma=False,
    )
```

```python
import functools
import math

import jax
import jax.numpy as jnp
import ml_dtypes
import numpy as np
from jax import lax
from jax.experimental import pallas as pl
from jax.experimental.pallas import tpu as pltpu
from jax.sharding import PartitionSpec as P

MESH = pl.DeviceIdType.MESH
F32, BF16 = jnp.float32, jnp.bfloat16


def tables(blocks, width):
    period = 2 * blocks * width
    odd = 2 * np.arange(blocks) + 1
    slot = np.arange(2 * blocks)
    angle = 2.0 * np.pi * (odd[:, None] * slot[None, :] % (4 * blocks)) / (4 * blocks)
    sign = np.where(slot < blocks, 1.0, -1.0)[None, :]
    outer = np.concatenate([np.cos(angle) * sign, -np.sin(angle) * sign], axis=0)
    angle = 2.0 * np.pi * (odd[:, None] * np.arange(width)[None, :]) / (2 * period)
    twist = np.stack([np.cos(angle), np.sin(angle)])
    spot = np.arange(width)
    angle = 2.0 * np.pi * (spot[:, None] * spot[None, :] % width) / width
    cos, sin = np.cos(angle), np.sin(angle)
    inner = np.block([[cos, -sin], [sin, cos]])
    back = np.block([[cos, sin], [-sin, cos]])
    mats = np.stack([outer, outer.T * (2.0 / period), inner, back])
    high = mats.astype(ml_dtypes.bfloat16)
    low = (mats - high.astype(np.float64)).astype(ml_dtypes.bfloat16)
    return np.stack([high, low], axis=1), twist.astype(np.float32)


def split(value):
    high = value.astype(BF16)
    return high, (value - high.astype(F32)).astype(BF16)


def dot(a, b):
    return jnp.dot(a, b, preferred_element_type=F32)


def dot3(a, b):
    return dot(a[0], b[0]) + dot(a[1], b[0]) + dot(a[0], b[1])


def fade_table(rate, freq, shift, lag, step, period):
    turns = freq * (lag * (1.0 / period)) + shift
    turns = turns - jnp.floor(turns)
    v = 4.0 * jnp.abs(turns - 0.5) - 1.0
    w = v * v
    poly = 0.00015148419 * w - 0.00467376557
    poly = poly * w + 0.07968967928
    poly = poly * w - 0.64596371106
    poly = poly * w + 1.57079631847
    return jnp.exp(-rate * (lag * step)) * (poly * v)


def kernel(n, modes, sig_ref, cot_ref, coef_ref, rate_ref, freq_ref, skip_ref, mat_ref, twist_ref,
           out_ref, gcoef_ref, gskip_ref,
           stage, send1, recv1, send2, recv2, kspec, through, corr_out, corr_own, corr_in, fades, direct,
           skip_mine, skip_mid, skip_all, skip_sum, skip_in, ssem, rsem):
    width = n
    core, me = lax.axis_index("dp"), lax.axis_index("seq")
    z, xy = lax.div(me, 16), lax.rem(me, 16)

    def remote(src, dst, k, seq=None):
        device = {"dp": 1 - core} if seq is None else {"seq": seq}
        return pltpu.make_async_remote_copy(
            src_ref=src, dst_ref=dst, send_sem=ssem.at[k], recv_sem=rsem.at[k], device_id=device,
            device_id_type=MESH)

    def finish(ref, k):
        pltpu.make_async_copy(ref, ref, ssem.at[k]).wait()
        pltpu.make_async_copy(ref, ref, rsem.at[k]).wait()

    barrier = pltpu.get_barrier_semaphore()

    def greet(i, c):
        pl.semaphore_signal(barrier, inc=1, device_id={"seq": lax.bitwise_xor(me, i)}, device_id_type=MESH)
        return c

    lax.fori_loop(1, n, greet, 0)
    pl.semaphore_signal(barrier, inc=1, device_id={"dp": 1 - core}, device_id_type=MESH)

    for k in range(8):
        src = (sig_ref, cot_ref)[k // 4]
        block = src[:, (k % 4) * width:(k % 4 + 1) * width].astype(F32)
        stage[pl.ds(k, n, stride=8), :] = block.T
    send1[...] = stage[...].reshape(n, 8, width).astype(BF16)

    pl.semaphore_wait(barrier, n)

    def post1(i, c):
        t = lax.bitwise_xor(me, i)
        remote(send1.at[t], recv1.at[me], 0, t).start()
        return c

    lax.fori_loop(1, n, post1, 0)
    recv1[me] = send1[me]

    lane = lax.broadcasted_iota(jnp.int32, (1, width), 1)
    wide = jnp.zeros((2 * modes, width), F32)
    slim = jnp.zeros((modes, width), F32)
    for j in range(4):
        for d in range(2):
            k = j * 2 + d
            cols = slice(j * width, (j + 1) * width)
            turn = lambda v, spot: pltpu.roll(v, lax.rem(spot + width - me, width), 1)
            wide = jnp.where(lane == k, turn(coef_ref[d, :, cols], k), wide)
            slim = jnp.where(lane == 8 + k, turn(rate_ref[d, :, cols], 8 + k), slim)
            slim = jnp.where(lane == 16 + k, turn(freq_ref[d, :, cols].astype(F32), 16 + k), slim)
    rows = jnp.where(lane < 8, wide, jnp.concatenate([slim, slim], axis=0)).T

    mat = lambda k: (mat_ref[k, 0], mat_ref[k, 1])
    outer, outer_t, inner, back = mat(0), mat(1), mat(2), mat(3)
    tcos, tsin = twist_ref[0], twist_ref[1]
    shift = jnp.where(lane < modes, 0.0, 0.75)
    spot = lax.broadcasted_iota(jnp.int32, (n, 1), 0).astype(F32)
    first = (lax.broadcasted_iota(jnp.int32, (n, width), 0) == 0) & (lax.broadcasted_iota(jnp.int32, (n, width), 1) == 0)
    scale = 2.0 * (modes * n * width) ** -0.5
    back_scale = scale

    def twisted(a):
        re, im = a[:n], a[n:]
        return jnp.concatenate([re * tcos + im * tsin, im * tcos - re * tsin], axis=1)

    for j in range(4):
        halves = []
        for d in range(2):
            k = j * 2 + d
            raw, rate, freq = rows[k:k + 1], rows[8 + k:9 + k] * (1.0 / (n * width)), rows[16 + k:17 + k]
            swap = jnp.concatenate([raw[:, modes:], raw[:, :modes]], axis=1)
            c1 = jnp.where(lane < modes, raw, -swap) * scale
            c2 = jnp.where(lane < modes, -swap, -raw) * scale
            fa = fade_table(rate, freq, shift, spot if d == 0 else (n - 1.0) - spot, float(width), float(n))
            fb = fade_table(rate, freq, shift, spot if d == 0 else width - spot, 1.0, float(n * width))
            fades[k, 0] = fa
            fades[k, 1] = fb
            mixed = c1 * fa + c2 * pltpu.roll(fa, modes, 1)
            a, b = split(mixed), split(fb)
            nt = lambda x, y: lax.dot_general(x, y, (((1,), (1,)), ((), ())), preferred_element_type=F32)
            half = nt(a[0], b[0]) + nt(a[1], b[0]) + nt(a[0], b[1])
            halves.append(half if d == 0 else jnp.where(first, 0.0, half))
        wave = jnp.concatenate(halves, axis=0)
        kspec[j] = dot3(split(twisted(dot3(outer, split(wave)))), inner)

    finish(recv1.at[pl.ds(0, n - 1)], 0)
    stage[...] = recv1[...].astype(F32).reshape(8 * n, width)
    outer_cat = jnp.concatenate([outer[0][:, :n], outer[1][:, :n]], axis=1)
    skip_row = jnp.zeros((1, width), F32)

    def channel(i, skip_row):
        j = lax.rem(2 * (1 - core) + i, 4)
        s = stage[pl.ds(j, n, stride=8), :]
        g = stage[pl.ds(j + 4, n, stride=8), :]
        total = jnp.sum(jnp.sum(s * g, axis=0, keepdims=True), axis=1, keepdims=True)
        skip_row = skip_row + jnp.where(lane == j, total, 0.0)
        x = jnp.concatenate([s, g], axis=1).astype(BF16)
        a = dot(outer_cat, jnp.concatenate([x, x], axis=0))
        both = jnp.concatenate([twisted(a[:, :width]), twisted(a[:, width:])], axis=0)
        spec = dot3(split(both), inner)
        sre, sim, gre, gim = spec[:n, :width], spec[:n, width:], spec[n:, :width], spec[n:, width:]
        kre, kim = kspec[j, :, :width], kspec[j, :, width:]
        through[j, :, :width] = gre * kre + gim * kim
        through[j, :, width:] = gim * kre - gre * kim
        corr_out[i, :, :width] = gre * sre + gim * sim
        corr_out[i, :, width:] = gim * sre - gre * sim
        gain = jnp.sum(jnp.where(lane == me, skip_ref[pl.ds(j, 1), :], 0.0), axis=1, keepdims=True)
        direct[j] = gain * g
        return skip_row

    skip_row = lax.fori_loop(0, 2, channel, skip_row)
    to_peer = remote(corr_out.at[pl.ds(0, 2)], corr_in, 1)
    to_peer.start()
    skip_row = lax.fori_loop(2, 4, channel, skip_row)

    skip_mine[...] = skip_row
    for i in range(1, 8):
        tz = lax.bitwise_xor(z, i)
        remote(skip_mine, skip_mid.at[z], 2, tz * 16 + xy).start()
    skip_mid[z] = skip_row

    def untwist(b):
        re, im = b[:, :width], b[:, width:]
        return jnp.concatenate([re * tcos - im * tsin, im * tcos + re * tsin], axis=0)

    b = dot3(split(through[...].reshape(4 * n, 2 * width)), back)
    cols = jnp.concatenate([untwist(b[j * n:(j + 1) * n]) for j in range(4)], axis=1)
    y = dot3((outer_t[0][:n], outer_t[1][:n]), split(cols))

    finish(skip_mid.at[pl.ds(0, 7)], 2)
    for i in range(1, 16):
        t = lax.bitwise_xor(xy, i)
        remote(skip_mid, skip_all.at[:, xy], 3, z * 16 + t).start()
    skip_all[:, xy] = skip_mid[...]

    to_peer.wait()
    corr = (corr_out[2:4] + corr_in[...]).reshape(2 * n, 2 * width)
    b = dot3(split(corr), back)
    cols = jnp.concatenate([untwist(b[:n]), untwist(b[n:])], axis=1)
    w = dot3(outer_t, split(cols))
    for jj in range(2):
        for d in range(2):
            k = (2 * core + jj) * 2 + d
            fa, fb = fades[k, 0], fades[k, 1]
            part = w[d * n:(d + 1) * n, jj * width:(jj + 1) * width]
            if d:
                part = jnp.where(first, 0.0, part)
            t = dot3(split(part), split(fb))
            p = jnp.sum(fa * t, axis=0, keepdims=True)
            q = jnp.sum(fa * pltpu.roll(t, modes, 1), axis=0, keepdims=True)
            p2 = jnp.concatenate([p[:, modes:], p[:, :modes]], axis=1)
            q2 = jnp.concatenate([q[:, modes:], q[:, :modes]], axis=1)
            row = jnp.where(lane < modes, p - p2, -(q + q2)) * back_scale
            stage[pl.ds(4 + jj * 2 + d, n, stride=8), :] = jnp.broadcast_to(row, (n, width))

    for j in range(4):
        stage[pl.ds(j, n, stride=8), :] = y[:, j * width:(j + 1) * width] + direct[j]
    send2[...] = stage[...].reshape(n, 8, width).astype(BF16)

    def post2(i, c):
        t = lax.bitwise_xor(me, i)
        remote(send2.at[t], recv2.at[me], 4, t).start()
        return c

    lax.fori_loop(1, n, post2, 0)
    recv2[me] = send2[me]

    finish(skip_all.at[:, pl.ds(0, 15)], 3)
    skip_sum[...] = skip_all[...].reshape(n, width).T[:8]
    skip_peer = remote(skip_sum, skip_in, 5)
    skip_peer.start()

    finish(recv2.at[pl.ds(0, n - 1)], 4)
    stage[...] = recv2[...].astype(F32).reshape(8 * n, width)
    for jj in range(2):
        for d in range(2):
            block = stage[pl.ds(4 + jj * 2 + d, n, stride=8), :].T
            gcoef_ref[d, :, pl.ds(pl.multiple_of((2 * core + jj) * width, width), width)] = block.astype(BF16)
    mine = gcoef_ref.at[:, :, pl.ds(pl.multiple_of(2 * core * width, 2 * width), 2 * width)]
    coef_peer = remote(mine, mine, 6)
    coef_peer.start()
    for j in range(4):
        out_ref[:, j * width:(j + 1) * width] = stage[pl.ds(j, n, stride=8), :].T.astype(BF16)
    skip_peer.wait()
    gskip_ref[...] = skip_sum[...] + skip_in[...]
    coef_peer.wait()


def on_device(signal, grad_out, mode_coef, decay_param, freq_index, skip_gain):
    n = lax.axis_size("seq")
    width, channels = signal.shape[1:]
    modes = decay_param.shape[1]
    mats, twist = tables(n, width)
    vmem = pl.BlockSpec(memory_space=pltpu.VMEM)
    out, gcoef, gskip = pl.pallas_call(
        functools.partial(kernel, n, modes),
        out_shape=(
            jax.ShapeDtypeStruct((width, channels), BF16),
            jax.ShapeDtypeStruct((2, 2 * modes, channels), BF16),
            jax.ShapeDtypeStruct((8, n), F32),
        ),
        in_specs=[vmem] * 8,
        out_specs=(vmem,) * 3,
        scratch_shapes=[
            pltpu.VMEM((8 * n, width), F32),
            pltpu.VMEM((n, 8, width), BF16),
            pltpu.VMEM((n, 8, width), BF16),
            pltpu.VMEM((n, 8, width), BF16),
            pltpu.VMEM((n, 8, width), BF16),
            pltpu.VMEM((4, n, 2 * width), F32),
            pltpu.VMEM((4, n, 2 * width), F32),
            pltpu.VMEM((4, n, 2 * width), F32),
            pltpu.VMEM((2, n, 2 * width), F32),
            pltpu.VMEM((2, n, 2 * width), F32),
            pltpu.VMEM((8, 2, n, 2 * modes), F32),
            pltpu.VMEM((4, n, width), F32),
            pltpu.VMEM((1, width), F32),
            pltpu.VMEM((8, 1, width), F32),
            pltpu.VMEM((8, 16, 1, width), F32),
            pltpu.VMEM((8, width), F32),
            pltpu.VMEM((8, width), F32),
            pltpu.SemaphoreType.DMA((8,)),
            pltpu.SemaphoreType.DMA((8,)),
        ],
        compiler_params=pltpu.CompilerParams(
            collective_id=0, has_side_effects=True, vmem_limit_bytes=40 * 1024 * 1024),
    )(signal[0], grad_out[0], mode_coef.reshape(2, 2 * modes, channels), decay_param, freq_index,
      skip_gain.reshape(channels // width, width), mats, twist)
    return (out[None], gcoef.astype(F32).reshape(mode_coef.shape), gskip[:channels // width].reshape(channels))


def solution(mesh):
    return jax.shard_map(
        on_device,
        mesh=mesh,
        in_specs=(P("dp", "seq", None), P("dp", "seq", None), P(), P(), P(), P()),
        out_specs=(P("dp", "seq", None), P(), P()),
        check_vma=False,
    )
```

```python
import functools

import jax
import jax.numpy as jnp
import ml_dtypes
import numpy as np
from jax import lax
from jax.experimental import pallas as pl
from jax.experimental.pallas import tpu as pltpu
from jax.sharding import PartitionSpec as P

MESH = pl.DeviceIdType.MESH
F32, BF16 = jnp.float32, jnp.bfloat16
ROOM = 62 * 1024 * 1024
UNROLL = 8


def tables(blocks, width):
    period = 2 * blocks * width
    odd = 2 * np.arange(blocks) + 1
    slot = np.arange(2 * blocks)
    angle = 2.0 * np.pi * (odd[:, None] * slot[None, :] % (4 * blocks)) / (4 * blocks)
    sign = np.where(slot < blocks, 1.0, -1.0)[None, :]
    outer = np.concatenate([np.cos(angle) * sign, -np.sin(angle) * sign], axis=0)
    angle = 2.0 * np.pi * (odd[:, None] * np.arange(width)[None, :]) / (2 * period)
    twist = np.stack([np.cos(angle), np.sin(angle)])
    spot = np.arange(width)
    angle = 2.0 * np.pi * (spot[:, None] * spot[None, :] % width) / width
    cos, sin = np.cos(angle), np.sin(angle)
    inner = np.block([[cos, -sin], [sin, cos]])
    back = np.block([[cos, sin], [-sin, cos]])
    mats = np.stack([outer, outer.T * (2.0 / period), inner, back])
    high = mats.astype(ml_dtypes.bfloat16)
    low = (mats - high.astype(np.float64)).astype(ml_dtypes.bfloat16)
    return np.stack([high, low], axis=1), twist.astype(np.float32)


def split(value):
    high = value.astype(BF16)
    return high, (value - high.astype(F32)).astype(BF16)


def dot(a, b):
    return jnp.dot(a, b, preferred_element_type=F32)


def dot3(a, b):
    return dot(a[0], b[0]) + dot(a[1], b[0]) + dot(a[0], b[1])


def fade_table(rate, freq, shift, lag, step, period):
    turns = freq * (lag * (1.0 / period)) + shift
    turns = turns - jnp.floor(turns)
    v = 4.0 * jnp.abs(turns - 0.5) - 1.0
    w = v * v
    poly = 0.00015148419 * w - 0.00467376557
    poly = poly * w + 0.07968967928
    poly = poly * w - 0.64596371106
    poly = poly * w + 1.57079631847
    return jnp.exp(-rate * (lag * step)) * (poly * v)


def kernel(n, modes, sig_in, cot_in, coef_in, rate_in, freq_in, gain_in, mat_in, twist_in,
           out_ref, gcoef_ref, gskip_ref,
           sig_ref, cot_ref, coef_ref, rate_ref, freq_ref, gain_ref, mat_ref, twist_ref, lsem,
           stage, stage2, send1, recv1, send2, recv2, kspec, through, corr_out, corr_in, fades, direct,
           gmid, gall, skip_sum, skip_in, ssem, rsem):
    width = n
    core, me = lax.axis_index("dp"), lax.axis_index("seq")
    z, xy = lax.div(me, 16), lax.rem(me, 16)

    loads = [
        pltpu.make_async_copy(src, dst, lsem.at[k]) for k, (src, dst) in enumerate((
            (sig_in, sig_ref), (cot_in, cot_ref), (coef_in, coef_ref), (rate_in, rate_ref), (freq_in, freq_ref),
            (gain_in, gain_ref), (mat_in, mat_ref), (twist_in, twist_ref)))]
    for load in loads:
        load.start()

    def remote(src, dst, k, seq=None):
        device = {"dp": 1 - core} if seq is None else {"seq": seq}
        return pltpu.make_async_remote_copy(
            src_ref=src, dst_ref=dst, send_sem=ssem.at[k], recv_sem=rsem.at[k], device_id=device,
            device_id_type=MESH)

    def finish(ref, k):
        pltpu.make_async_copy(ref, ref, ssem.at[k]).wait()
        pltpu.make_async_copy(ref, ref, rsem.at[k]).wait()

    barrier = pltpu.get_barrier_semaphore()

    def greet(i, c):
        pl.semaphore_signal(barrier, inc=1, device_id={"seq": lax.bitwise_xor(me, i)}, device_id_type=MESH)
        return c

    lax.fori_loop(1, n, greet, 0, unroll=UNROLL)
    pl.semaphore_signal(barrier, inc=1, device_id={"dp": 1 - core}, device_id_type=MESH)

    loads[0].wait()
    loads[1].wait()
    for k in range(8):
        src = (sig_ref, cot_ref)[k // 4]
        block = src[:, (k % 4) * width:(k % 4 + 1) * width].astype(F32)
        stage[pl.ds(k, n, stride=8), :] = block.T
    send1[...] = stage[...].reshape(n, 8, width).astype(BF16)

    pl.semaphore_wait(barrier, n)

    def post1(i, c):
        t = lax.bitwise_xor(me, i)
        remote(send1.at[t], recv1.at[me], 0, t).start()
        return c

    lax.fori_loop(1, n, post1, 0, unroll=UNROLL)
    recv1[me] = send1[me]

    for load in loads[2:]:
        load.wait()
    lane = lax.broadcasted_iota(jnp.int32, (1, width), 1)
    wide = jnp.zeros((2 * modes, width), F32)
    slim = jnp.zeros((modes, width), F32)
    for j in range(4):
        for d in range(2):
            k = j * 2 + d
            cols = slice(j * width, (j + 1) * width)
            turn = lambda v, spot: pltpu.roll(v, lax.rem(spot + width - me, width), 1)
            wide = jnp.where(lane == k, turn(coef_ref[d, :, cols], k), wide)
            slim = jnp.where(lane == 8 + k, turn(rate_ref[d, :, cols], 8 + k), slim)
            slim = jnp.where(lane == 16 + k, turn(freq_ref[d, :, cols].astype(F32), 16 + k), slim)
    rows = jnp.where(lane < 8, wide, jnp.concatenate([slim, slim], axis=0)).T

    mat = lambda k: (mat_ref[k, 0], mat_ref[k, 1])
    outer, outer_t, inner, back = mat(0), mat(1), mat(2), mat(3)
    tcos, tsin = twist_ref[0], twist_ref[1]
    shift = jnp.where(lane < modes, 0.0, 0.75)
    spot = lax.broadcasted_iota(jnp.int32, (n, 1), 0).astype(F32)
    first = (lax.broadcasted_iota(jnp.int32, (n, width), 0) == 0) & (
        lax.broadcasted_iota(jnp.int32, (n, width), 1) == 0)
    scale = 2.0 * (modes * n * width) ** -0.5

    def twisted(a):
        re, im = a[:n], a[n:]
        return jnp.concatenate([re * tcos + im * tsin, im * tcos - re * tsin], axis=1)

    def untwist(b):
        re, im = b[:, :width], b[:, width:]
        return jnp.concatenate([re * tcos - im * tsin, im * tcos + re * tsin], axis=0)

    for j in range(4):
        halves = []
        for d in range(2):
            k = j * 2 + d
            raw, rate, freq = rows[k:k + 1], rows[8 + k:9 + k] * (1.0 / (n * width)), rows[16 + k:17 + k]
            swap = jnp.concatenate([raw[:, modes:], raw[:, :modes]], axis=1)
            c1 = jnp.where(lane < modes, raw, -swap) * scale
            c2 = jnp.where(lane < modes, -swap, -raw) * scale
            fa = fade_table(rate, freq, shift, spot if d == 0 else (n - 1.0) - spot, float(width), float(n))
            fb = fade_table(rate, freq, shift, spot if d == 0 else width - spot, 1.0, float(n * width))
            fades[k, 0] = fa
            fades[k, 1] = fb
            mixed = c1 * fa + c2 * pltpu.roll(fa, modes, 1)
            a, b = split(mixed), split(fb)
            nt = lambda x, y: lax.dot_general(x, y, (((1,), (1,)), ((), ())), preferred_element_type=F32)
            half = nt(a[0], b[0]) + nt(a[1], b[0]) + nt(a[0], b[1])
            halves.append(half if d == 0 else jnp.where(first, 0.0, half))
        wave = jnp.concatenate(halves, axis=0)
        kspec[j] = dot3(split(twisted(dot3(outer, split(wave)))), inner)

    finish(recv1.at[pl.ds(0, n - 1)], 0)
    stage[...] = recv1[...].astype(F32).reshape(8 * n, width)
    outer_cat = jnp.concatenate([outer[0][:, :n], outer[1][:, :n]], axis=1)

    def channel(i, skip_row):
        j = lax.rem(2 * (1 - core) + i, 4)
        s = stage[pl.ds(j, n, stride=8), :]
        g = stage[pl.ds(j + 4, n, stride=8), :]
        total = jnp.sum(jnp.sum(s * g, axis=0, keepdims=True), axis=1, keepdims=True)
        skip_row = skip_row + jnp.where(lane == j, total, 0.0)
        x = jnp.concatenate([s, g], axis=1).astype(BF16)
        a = dot(outer_cat, jnp.concatenate([x, x], axis=0))
        both = jnp.concatenate([twisted(a[:, :width]), twisted(a[:, width:])], axis=0)
        spec = dot3(split(both), inner)
        sre, sim, gre, gim = spec[:n, :width], spec[:n, width:], spec[n:, :width], spec[n:, width:]
        kre, kim = kspec[j, :, :width], kspec[j, :, width:]
        through[j, :, :width] = gre * kre + gim * kim
        through[j, :, width:] = gim * kre - gre * kim
        corr_out[i, :, :width] = gre * sre + gim * sim
        corr_out[i, :, width:] = gim * sre - gre * sim
        gain = jnp.sum(jnp.where(lane == me, gain_ref[pl.ds(j, 1), :], 0.0), axis=1, keepdims=True)
        direct[j] = gain * g
        return skip_row

    skip_row = jnp.zeros((1, width), F32)
    for i in range(2):
        skip_row = channel(i, skip_row)
    to_peer = remote(corr_out.at[pl.ds(0, 2)], corr_in, 1)
    to_peer.start()
    for i in range(2, 4):
        skip_row = channel(i, skip_row)

    b = dot3(split(through[...].reshape(4 * n, 2 * width)), back)
    cols = jnp.concatenate([untwist(b[j * n:(j + 1) * n]) for j in range(4)], axis=1)
    y = dot3((outer_t[0][:n], outer_t[1][:n]), split(cols))
    for j in range(4):
        send2[:, j, :] = (y[:, j * width:(j + 1) * width] + direct[j]).astype(BF16)

    to_peer.wait()
    corr = (corr_out[2:4] + corr_in[...]).reshape(2 * n, 2 * width)
    b = dot3(split(corr), back)
    cols = jnp.concatenate([untwist(b[:n]), untwist(b[n:])], axis=1)
    w = dot3(outer_t, split(cols))
    grads = []
    for jj in range(2):
        for d in range(2):
            k = (2 * core + jj) * 2 + d
            fa, fb = fades[k, 0], fades[k, 1]
            part = w[d * n:(d + 1) * n, jj * width:(jj + 1) * width]
            if d:
                part = jnp.where(first, 0.0, part)
            t = dot3(split(part), split(fb))
            p = jnp.sum(fa * t, axis=0, keepdims=True)
            q = jnp.sum(fa * pltpu.roll(t, modes, 1), axis=0, keepdims=True)
            p2 = jnp.concatenate([p[:, modes:], p[:, :modes]], axis=1)
            q2 = jnp.concatenate([q[:, modes:], q[:, :modes]], axis=1)
            grads.append(jnp.where(lane < modes, p - p2, -(q + q2)) * scale)
    skip_high = skip_row.astype(BF16).astype(F32)
    blank = jnp.zeros((2, width), F32)
    gmid[z] = jnp.concatenate(grads + [skip_high, skip_row - skip_high, blank], axis=0).astype(BF16)

    for i in range(1, 8):
        remote(gmid.at[z], gmid.at[z], 2, lax.bitwise_xor(z, i) * 16 + xy).start()

    def post2(i, c):
        t = lax.bitwise_xor(me, i)
        remote(send2.at[t], recv2.at[me], 4, t).start()
        return c

    lax.fori_loop(64, n, post2, 0, unroll=UNROLL)
    finish(gmid.at[pl.ds(0, 7)], 2)
    for i in range(1, 16):
        remote(gmid, gall.at[:, xy], 3, z * 16 + lax.bitwise_xor(xy, i)).start()
    lax.fori_loop(1, 64, post2, 0, unroll=UNROLL)
    recv2[me] = send2[me]
    gall[:, xy] = gmid[...]

    finish(gall.at[:, pl.ds(0, 15)], 3)
    stage2[...] = gall[...].astype(F32).reshape(8 * n, width)
    skip_sum[...] = (stage2[pl.ds(4, n, stride=8), :] + stage2[pl.ds(5, n, stride=8), :]).T[:4]
    for jj in range(2):
        for d in range(2):
            block = stage2[pl.ds(jj * 2 + d, n, stride=8), :].T
            gcoef_ref[d, :, pl.ds(pl.multiple_of((2 * core + jj) * width, width), width)] = block.astype(BF16)
    skip_peer = remote(skip_sum, skip_in, 5)
    skip_peer.start()
    mine = gcoef_ref.at[:, :, pl.ds(pl.multiple_of(2 * core * width, 2 * width), 2 * width)]
    coef_peer = remote(mine, mine, 6)
    coef_peer.start()

    finish(recv2.at[pl.ds(0, n - 1)], 4)
    for j in range(4):
        out_ref[:, j * width:(j + 1) * width] = recv2[:, j, :].astype(F32).T.astype(BF16)
    skip_peer.wait()
    gskip_ref[...] = skip_sum[...] + skip_in[...]
    coef_peer.wait()


def finals(out_in, gcoef_in, gskip_in, out_ref, gcoef_ref, gskip_ref):
    out_ref[...] = out_in[...]
    gcoef_ref[...] = gcoef_in[...].astype(F32)
    gskip_ref[...] = gskip_in[...]


def on_device(signal, grad_out, mode_coef, decay_param, freq_index, skip_gain):
    n = lax.axis_size("seq")
    width, channels = signal.shape[1:]
    modes = decay_param.shape[1]
    mats, twist = tables(n, width)
    vmem = pl.BlockSpec(memory_space=pltpu.VMEM)
    operands = (signal[0], grad_out[0], mode_coef.reshape(2, 2 * modes, channels), decay_param, freq_index,
                skip_gain.reshape(channels // width, width), mats, twist)
    out = pl.pallas_call(
        functools.partial(kernel, n, modes),
        out_shape=(
            jax.ShapeDtypeStruct((width, channels), BF16),
            jax.ShapeDtypeStruct((2, 2 * modes, channels), BF16),
            jax.ShapeDtypeStruct((channels // width, n), F32),
        ),
        in_specs=[pl.BlockSpec(memory_space=pl.ANY)] * 8,
        out_specs=(vmem,) * 3,
        scratch_shapes=[pltpu.VMEM(t.shape, t.dtype) for t in operands] + [
            pltpu.SemaphoreType.DMA((8,)),
            pltpu.VMEM((8 * n, width), F32),
            pltpu.VMEM((8 * n, width), F32),
            pltpu.VMEM((n, 8, width), BF16),
            pltpu.VMEM((n, 8, width), BF16),
            pltpu.VMEM((n, 4, width), BF16),
            pltpu.VMEM((n, 4, width), BF16),
            pltpu.VMEM((4, n, 2 * width), F32),
            pltpu.VMEM((4, n, 2 * width), F32),
            pltpu.VMEM((4, n, 2 * width), F32),
            pltpu.VMEM((2, n, 2 * width), F32),
            pltpu.VMEM((8, 2, n, 2 * modes), F32),
            pltpu.VMEM((4, n, width), F32),
            pltpu.VMEM((8, 8, width), BF16),
            pltpu.VMEM((8, 16, 8, width), BF16),
            pltpu.VMEM((4, width), F32),
            pltpu.VMEM((4, width), F32),
            pltpu.SemaphoreType.DMA((8,)),
            pltpu.SemaphoreType.DMA((8,)),
        ],
        compiler_params=pltpu.CompilerParams(
            collective_id=0, has_side_effects=True, vmem_limit_bytes=ROOM),
    )(*operands)
    out = pl.pallas_call(
        finals,
        out_shape=tuple(jax.ShapeDtypeStruct(t.shape, d) for t, d in zip(out, (BF16, F32, F32))),
        in_specs=[vmem] * 3,
        out_specs=(vmem,) * 3,
        compiler_params=pltpu.CompilerParams(vmem_limit_bytes=ROOM),
    )(*out)
    return (out[0][None], out[1].reshape(mode_coef.shape), out[2].reshape(channels))


def solution(mesh):
    return jax.shard_map(
        on_device,
        mesh=mesh,
        in_specs=(P("dp", "seq", None), P("dp", "seq", None), P(), P(), P(), P()),
        out_specs=(P("dp", "seq", None), P(), P()),
        check_vma=False,
    )
```

```python
import functools

import jax
import jax.numpy as jnp
import ml_dtypes
import numpy as np
from jax import lax
from jax.experimental import pallas as pl
from jax.experimental.pallas import tpu as pltpu
from jax.sharding import PartitionSpec as P

MESH = pl.DeviceIdType.MESH
F32, BF16 = jnp.float32, jnp.bfloat16
ROOM = 62 * 1024 * 1024
UNROLL = 8
FAR_FIRST = (4, 5, 3, 7, 2, 6, 1, 0)


def tables(blocks, width):
    period = 2 * blocks * width
    odd = 2 * np.arange(blocks) + 1
    slot = np.arange(2 * blocks)
    angle = 2.0 * np.pi * (odd[:, None] * slot[None, :] % (4 * blocks)) / (4 * blocks)
    sign = np.where(slot < blocks, 1.0, -1.0)[None, :]
    outer = np.concatenate([np.cos(angle) * sign, -np.sin(angle) * sign], axis=0)
    angle = 2.0 * np.pi * (odd[:, None] * np.arange(width)[None, :]) / (2 * period)
    twist = np.stack([np.cos(angle), np.sin(angle)])
    spot = np.arange(width)
    angle = 2.0 * np.pi * (spot[:, None] * spot[None, :] % width) / width
    cos, sin = np.cos(angle), np.sin(angle)
    inner = np.block([[cos, -sin], [sin, cos]])
    back = np.block([[cos, sin], [-sin, cos]])
    mats = np.stack([outer, outer.T * (2.0 / period), inner, back])
    high = mats.astype(ml_dtypes.bfloat16)
    low = (mats - high.astype(np.float64)).astype(ml_dtypes.bfloat16)
    return np.stack([high, low], axis=1), twist.astype(np.float32)


def split(value):
    high = value.astype(BF16)
    return high, (value - high.astype(F32)).astype(BF16)


def dot(a, b):
    return jnp.dot(a, b, preferred_element_type=F32)


def dot3(a, b):
    return dot(a[0], b[0]) + dot(a[1], b[0]) + dot(a[0], b[1])


def fade_table(rate, freq, shift, lag, step, period):
    turns = freq * (lag * (1.0 / period)) + shift
    turns = turns - jnp.floor(turns)
    v = 4.0 * jnp.abs(turns - 0.5) - 1.0
    w = v * v
    poly = 0.00015148419 * w - 0.00467376557
    poly = poly * w + 0.07968967928
    poly = poly * w - 0.64596371106
    poly = poly * w + 1.57079631847
    return jnp.exp(-rate * (lag * step)) * (poly * v)


def kernel(n, modes, sig_in, cot_in, coef_in, rate_in, freq_in, gain_in, mat_in, twist_in,
           out_ref, gcoef_ref, gskip_ref,
           sig_ref, cot_ref, coef_ref, rate_ref, freq_ref, gain_ref, mat_ref, twist_ref, lsem,
           stage, stage2, send1, recv1, send2, recv2, kspec, through, corr_out, corr_in, fades, direct,
           gmid, gsend, gall, ssem, rsem):
    width = n
    core, me = lax.axis_index("dp"), lax.axis_index("seq")
    z, xy = lax.div(me, 16), lax.rem(me, 16)

    loads = [
        pltpu.make_async_copy(src, dst, lsem.at[k]) for k, (src, dst) in enumerate((
            (sig_in, sig_ref), (cot_in, cot_ref), (coef_in, coef_ref), (rate_in, rate_ref), (freq_in, freq_ref),
            (gain_in, gain_ref), (mat_in, mat_ref), (twist_in, twist_ref)))]
    for load in loads:
        load.start()

    def remote(src, dst, k, seq=None, other=False):
        device = {} if seq is None else {"seq": seq}
        if other:
            device["dp"] = 1 - core
        return pltpu.make_async_remote_copy(
            src_ref=src, dst_ref=dst, send_sem=ssem.at[k], recv_sem=rsem.at[k], device_id=device,
            device_id_type=MESH)

    def finish(ref, k):
        pltpu.make_async_copy(ref, ref, ssem.at[k]).wait()
        pltpu.make_async_copy(ref, ref, rsem.at[k]).wait()

    barrier = pltpu.get_barrier_semaphore()

    def greet(i, c):
        pl.semaphore_signal(barrier, inc=1, device_id={"seq": lax.bitwise_xor(me, i)}, device_id_type=MESH)
        return c

    lax.fori_loop(1, n, greet, 0, unroll=UNROLL)
    for i in range(8):
        pl.semaphore_signal(
            barrier, inc=1, device_id={"dp": 1 - core, "seq": lax.bitwise_xor(z, i) * 16 + xy}, device_id_type=MESH)

    loads[0].wait()
    loads[1].wait()
    for k in range(8):
        src = (sig_ref, cot_ref)[k // 4]
        block = src[:, (k % 4) * width:(k % 4 + 1) * width].astype(F32)
        stage[pl.ds(k, n, stride=8), :] = block.T
    send1[...] = stage[...].reshape(n, 8, width).astype(BF16)

    pl.semaphore_wait(barrier, n + 7)

    def post1(i, c):
        t = lax.bitwise_xor(me, i)
        remote(send1.at[t], recv1.at[me], 0, t).start()
        return c

    for q in FAR_FIRST:
        lax.fori_loop(max(16 * q, 1), 16 * q + 16, post1, 0, unroll=UNROLL)
    recv1[me] = send1[me]

    for load in loads[2:]:
        load.wait()
    lane = lax.broadcasted_iota(jnp.int32, (1, width), 1)
    wide = jnp.zeros((2 * modes, width), F32)
    slim = jnp.zeros((modes, width), F32)
    for j in range(4):
        for d in range(2):
            k = j * 2 + d
            cols = slice(j * width, (j + 1) * width)
            turn = lambda v, spot: pltpu.roll(v, lax.rem(spot + width - me, width), 1)
            wide = jnp.where(lane == k, turn(coef_ref[d, :, cols], k), wide)
            slim = jnp.where(lane == 8 + k, turn(rate_ref[d, :, cols], 8 + k), slim)
            slim = jnp.where(lane == 16 + k, turn(freq_ref[d, :, cols].astype(F32), 16 + k), slim)
    rows = jnp.where(lane < 8, wide, jnp.concatenate([slim, slim], axis=0)).T

    mat = lambda k: (mat_ref[k, 0], mat_ref[k, 1])
    outer, outer_t, inner, back = mat(0), mat(1), mat(2), mat(3)
    tcos, tsin = twist_ref[0], twist_ref[1]
    shift = jnp.where(lane < modes, 0.0, 0.75)
    spot = lax.broadcasted_iota(jnp.int32, (n, 1), 0).astype(F32)
    first = (lax.broadcasted_iota(jnp.int32, (n, width), 0) == 0) & (
        lax.broadcasted_iota(jnp.int32, (n, width), 1) == 0)
    scale = 2.0 * (modes * n * width) ** -0.5

    def twisted(a):
        re, im = a[:n], a[n:]
        return jnp.concatenate([re * tcos + im * tsin, im * tcos - re * tsin], axis=1)

    def untwist(b):
        re, im = b[:, :width], b[:, width:]
        return jnp.concatenate([re * tcos - im * tsin, im * tcos + re * tsin], axis=0)

    for j in range(4):
        halves = []
        for d in range(2):
            k = j * 2 + d
            raw, rate, freq = rows[k:k + 1], rows[8 + k:9 + k] * (1.0 / (n * width)), rows[16 + k:17 + k]
            swap = jnp.concatenate([raw[:, modes:], raw[:, :modes]], axis=1)
            c1 = jnp.where(lane < modes, raw, -swap) * scale
            c2 = jnp.where(lane < modes, -swap, -raw) * scale
            fa = fade_table(rate, freq, shift, spot if d == 0 else (n - 1.0) - spot, float(width), float(n))
            fb = fade_table(rate, freq, shift, spot if d == 0 else width - spot, 1.0, float(n * width))
            fades[k, 0] = fa
            fades[k, 1] = fb
            mixed = c1 * fa + c2 * pltpu.roll(fa, modes, 1)
            a, b = split(mixed), split(fb)
            nt = lambda x, y: lax.dot_general(x, y, (((1,), (1,)), ((), ())), preferred_element_type=F32)
            half = nt(a[0], b[0]) + nt(a[1], b[0]) + nt(a[0], b[1])
            halves.append(half if d == 0 else jnp.where(first, 0.0, half))
        wave = jnp.concatenate(halves, axis=0)
        kspec[j] = dot3(split(twisted(dot3(outer, split(wave)))), inner)

    finish(recv1.at[pl.ds(0, n - 1)], 0)
    stage[...] = recv1[...].astype(F32).reshape(8 * n, width)
    outer_cat = jnp.concatenate([outer[0][:, :n], outer[1][:, :n]], axis=1)

    def channel(i, skip_row):
        j = lax.rem(2 * (1 - core) + i, 4)
        s = stage[pl.ds(j, n, stride=8), :]
        g = stage[pl.ds(j + 4, n, stride=8), :]
        total = jnp.sum(jnp.sum(s * g, axis=0, keepdims=True), axis=1, keepdims=True)
        skip_row = skip_row + jnp.where(lane == j, total, 0.0)
        x = jnp.concatenate([s, g], axis=1).astype(BF16)
        a = dot(outer_cat, jnp.concatenate([x, x], axis=0))
        both = jnp.concatenate([twisted(a[:, :width]), twisted(a[:, width:])], axis=0)
        spec = dot3(split(both), inner)
        sre, sim, gre, gim = spec[:n, :width], spec[:n, width:], spec[n:, :width], spec[n:, width:]
        kre, kim = kspec[j, :, :width], kspec[j, :, width:]
        through[j, :, :width] = gre * kre + gim * kim
        through[j, :, width:] = gim * kre - gre * kim
        corr_out[i, :, :width] = gre * sre + gim * sim
        corr_out[i, :, width:] = gim * sre - gre * sim
        gain = jnp.sum(jnp.where(lane == me, gain_ref[pl.ds(j, 1), :], 0.0), axis=1, keepdims=True)
        direct[j] = gain * g
        return skip_row

    skip_row = jnp.zeros((1, width), F32)
    for i in range(2):
        skip_row = channel(i, skip_row)
    to_peer = remote(corr_out.at[pl.ds(0, 2)], corr_in, 1, None, True)
    to_peer.start()
    for i in range(2, 4):
        skip_row = channel(i, skip_row)

    to_peer.wait()
    corr = (corr_out[2:4] + corr_in[...]).reshape(2 * n, 2 * width)
    b = dot3(split(corr), back)
    cols = jnp.concatenate([untwist(b[:n]), untwist(b[n:])], axis=1)
    w = dot3(outer_t, split(cols))
    grads = []
    for jj in range(2):
        for d in range(2):
            k = (2 * core + jj) * 2 + d
            fa, fb = fades[k, 0], fades[k, 1]
            part = w[d * n:(d + 1) * n, jj * width:(jj + 1) * width]
            if d:
                part = jnp.where(first, 0.0, part)
            t = dot3(split(part), split(fb))
            p = jnp.sum(fa * t, axis=0, keepdims=True)
            q = jnp.sum(fa * pltpu.roll(t, modes, 1), axis=0, keepdims=True)
            p2 = jnp.concatenate([p[:, modes:], p[:, :modes]], axis=1)
            q2 = jnp.concatenate([q[:, modes:], q[:, :modes]], axis=1)
            grads.append(jnp.where(lane < modes, p - p2, -(q + q2)) * scale)
    skip_high = skip_row.astype(BF16).astype(F32)
    blank = jnp.zeros((2, width), F32)
    slot = core * 8 + z
    gmid[slot] = jnp.concatenate(grads + [skip_high, skip_row - skip_high, blank], axis=0).astype(BF16)

    for i in range(1, 8):
        for other in (False, True):
            remote(gmid.at[slot], gmid.at[slot], 2, lax.bitwise_xor(z, i) * 16 + xy, other).start()
    remote(gmid.at[slot], gmid.at[slot], 2, None, True).start()
    b = dot3(split(through[...].reshape(4 * n, 2 * width)), back)
    cols = jnp.concatenate([untwist(b[j * n:(j + 1) * n]) for j in range(4)], axis=1)
    y = dot3((outer_t[0][:n], outer_t[1][:n]), split(cols))
    for j in range(4):
        stage2[pl.ds(j, n, stride=4), :] = y[:, j * width:(j + 1) * width] + direct[j]
    send2[...] = stage2[:4 * n].reshape(n, 4, width).astype(BF16)

    def post2(i, c):
        t = lax.bitwise_xor(me, i)
        remote(send2.at[t], recv2.at[me], 4, t).start()
        return c

    for q in FAR_FIRST[:8]:
        lax.fori_loop(max(16 * q, 1), 16 * q + 16, post2, 0, unroll=UNROLL)
    finish(gmid.at[pl.ds(0, 15)], 2)
    seen = gmid[...].astype(F32)
    gsend[pl.ds(0, 16)] = seen[:, :4].astype(BF16)
    skips = jnp.zeros((2, width), F32)
    for q in range(8):
        part = seen[q, 4:5] + seen[q, 5:6] + (seen[8 + q, 4:5] + seen[8 + q, 5:6])
        part = pltpu.roll(part, 4 * q, 1) if q else part
        high = part.astype(BF16).astype(F32)
        skips = skips + jnp.concatenate([high, part - high], axis=0)
    gsend[16] = jnp.concatenate([skips, blank], axis=0).astype(BF16)
    for i in range(1, 16):
        remote(gsend, gall.at[xy], 3, z * 16 + lax.bitwise_xor(xy, i)).start()
    for q in FAR_FIRST[8:]:
        lax.fori_loop(max(16 * q, 1), 16 * q + 16, post2, 0, unroll=UNROLL)
    recv2[me] = send2[me]
    gall[xy] = gsend[...]

    finish(gall.at[pl.ds(0, 15)], 3)
    stage2[...] = gall[...].astype(F32).reshape(17 * 64, width)
    skips = (stage2[pl.ds(64, 16, stride=68), :] + stage2[pl.ds(65, 16, stride=68), :]).T
    gskip_ref[...] = jnp.concatenate([skips[4 * q:4 * q + 4] for q in range(8)], axis=1)
    for c in range(2):
        for jj in range(2):
            for d in range(2):
                block = jnp.concatenate([
                    stage2[pl.ds((8 * c + q) * 4 + jj * 2 + d, 16, stride=68), :] for q in range(8)], axis=0).T
                cols = slice((2 * c + jj) * width, (2 * c + jj + 1) * width)
                gcoef_ref[d, :, cols] = block.astype(BF16)
    finish(recv2.at[pl.ds(0, n - 1)], 4)
    stage[:4 * n] = recv2[...].astype(F32).reshape(4 * n, width)
    for j in range(4):
        out_ref[:, j * width:(j + 1) * width] = stage[pl.ds(j, n, stride=4), :].T.astype(BF16)


def finals(out_in, gcoef_in, gskip_in, out_ref, gcoef_ref, gskip_ref):
    out_ref[...] = out_in[...]
    gcoef_ref[...] = gcoef_in[...].astype(F32)
    gskip_ref[...] = gskip_in[...]


def on_device(signal, grad_out, mode_coef, decay_param, freq_index, skip_gain):
    n = lax.axis_size("seq")
    width, channels = signal.shape[1:]
    modes = decay_param.shape[1]
    mats, twist = tables(n, width)
    vmem = pl.BlockSpec(memory_space=pltpu.VMEM)
    operands = (signal[0], grad_out[0], mode_coef.reshape(2, 2 * modes, channels), decay_param, freq_index,
                skip_gain.reshape(channels // width, width), mats, twist)
    out = pl.pallas_call(
        functools.partial(kernel, n, modes),
        out_shape=(
            jax.ShapeDtypeStruct((width, channels), BF16),
            jax.ShapeDtypeStruct((2, 2 * modes, channels), BF16),
            jax.ShapeDtypeStruct((channels // width, n), F32),
        ),
        in_specs=[pl.BlockSpec(memory_space=pl.ANY)] * 8,
        out_specs=(vmem,) * 3,
        scratch_shapes=[pltpu.VMEM(t.shape, t.dtype) for t in operands] + [
            pltpu.SemaphoreType.DMA((8,)),
            pltpu.VMEM((8 * n, width), F32),
            pltpu.VMEM((17 * 64, width), F32),
            pltpu.VMEM((n, 8, width), BF16),
            pltpu.VMEM((n, 8, width), BF16),
            pltpu.VMEM((n, 4, width), BF16),
            pltpu.VMEM((n, 4, width), BF16),
            pltpu.VMEM((4, n, 2 * width), F32),
            pltpu.VMEM((4, n, 2 * width), F32),
            pltpu.VMEM((4, n, 2 * width), F32),
            pltpu.VMEM((2, n, 2 * width), F32),
            pltpu.VMEM((8, 2, n, 2 * modes), F32),
            pltpu.VMEM((4, n, width), F32),
            pltpu.VMEM((16, 8, width), BF16),
            pltpu.VMEM((17, 4, width), BF16),
            pltpu.VMEM((16, 17, 4, width), BF16),
            pltpu.SemaphoreType.DMA((8,)),
            pltpu.SemaphoreType.DMA((8,)),
        ],
        compiler_params=pltpu.CompilerParams(
            collective_id=0, has_side_effects=True, vmem_limit_bytes=ROOM),
    )(*operands)
    out = pl.pallas_call(
        finals,
        out_shape=tuple(jax.ShapeDtypeStruct(t.shape, d) for t, d in zip(out, (BF16, F32, F32))),
        in_specs=[vmem] * 3,
        out_specs=(vmem,) * 3,
        compiler_params=pltpu.CompilerParams(vmem_limit_bytes=ROOM),
    )(*out)
    return (out[0][None], out[1].reshape(mode_coef.shape), out[2].reshape(channels))


def solution(mesh):
    return jax.shard_map(
        on_device,
        mesh=mesh,
        in_specs=(P("dp", "seq", None), P("dp", "seq", None), P(), P(), P(), P()),
        out_specs=(P("dp", "seq", None), P(), P()),
        check_vma=False,
    )
```

```python
import functools

import jax
import jax.numpy as jnp
import ml_dtypes
import numpy as np
from jax import lax
from jax.experimental import pallas as pl
from jax.experimental.pallas import tpu as pltpu
from jax.sharding import PartitionSpec as P

MESH = pl.DeviceIdType.MESH
F32, BF16 = jnp.float32, jnp.bfloat16
ROOM = 62 * 1024 * 1024
UNROLL = 8
FAR_FIRST = (4, 5, 3, 7, 2, 6, 1, 0)


def tables(blocks, width):
    period = 2 * blocks * width
    odd = 2 * np.arange(blocks) + 1
    slot = np.arange(2 * blocks)
    angle = 2.0 * np.pi * (odd[:, None] * slot[None, :] % (4 * blocks)) / (4 * blocks)
    sign = np.where(slot < blocks, 1.0, -1.0)[None, :]
    outer = np.concatenate([np.cos(angle) * sign, -np.sin(angle) * sign], axis=0)
    angle = 2.0 * np.pi * (odd[:, None] * np.arange(width)[None, :]) / (2 * period)
    twist = np.stack([np.cos(angle), np.sin(angle)])
    spot = np.arange(width)
    angle = 2.0 * np.pi * (spot[:, None] * spot[None, :] % width) / width
    cos, sin = np.cos(angle), np.sin(angle)
    inner = np.block([[cos, -sin], [sin, cos]])
    back = np.block([[cos, sin], [-sin, cos]])
    mats = np.stack([outer, outer.T * (2.0 / period), inner, back])
    high = mats.astype(ml_dtypes.bfloat16)
    low = (mats - high.astype(np.float64)).astype(ml_dtypes.bfloat16)
    return np.stack([high, low], axis=1), twist.astype(np.float32)


def split(value):
    high = value.astype(BF16)
    return high, (value - high.astype(F32)).astype(BF16)


def dot(a, b):
    return jnp.dot(a, b, preferred_element_type=F32)


def dot3(a, b):
    return dot(a[0], b[0]) + dot(a[1], b[0]) + dot(a[0], b[1])


def fade_table(rate, freq, shift, lag, step, period):
    turns = freq * (lag * (1.0 / period)) + shift
    turns = turns - jnp.floor(turns)
    v = 4.0 * jnp.abs(turns - 0.5) - 1.0
    w = v * v
    poly = 0.00015148419 * w - 0.00467376557
    poly = poly * w + 0.07968967928
    poly = poly * w - 0.64596371106
    poly = poly * w + 1.57079631847
    return jnp.exp(-rate * (lag * step)) * (poly * v)


def kernel(n, modes, sig_in, cot_in, coef_in, rate_in, freq_in, gain_in, mat_in, twist_in,
           out_ref, gcoef_ref, gskip_ref,
           sig_ref, cot_ref, coef_ref, rate_ref, freq_ref, gain_ref, mat_ref, twist_ref, lsem,
           stage, stage2, send1, recv1, send2, recv2, kspec, through, corr_out, corr_in, fades, direct,
           gmid, gsend, gall, ssem, rsem):
    width = n
    core, me = lax.axis_index("dp"), lax.axis_index("seq")
    z, xy = lax.div(me, 16), lax.rem(me, 16)

    loads = [
        pltpu.make_async_copy(src, dst, lsem.at[k]) for k, (src, dst) in enumerate((
            (sig_in, sig_ref), (cot_in, cot_ref), (coef_in, coef_ref), (rate_in, rate_ref), (freq_in, freq_ref),
            (gain_in, gain_ref), (mat_in, mat_ref), (twist_in, twist_ref)))]
    for load in loads:
        load.start()

    def remote(src, dst, k, seq=None, other=False):
        device = {} if seq is None else {"seq": seq}
        if other:
            device["dp"] = 1 - core
        return pltpu.make_async_remote_copy(
            src_ref=src, dst_ref=dst, send_sem=ssem.at[k], recv_sem=rsem.at[k], device_id=device,
            device_id_type=MESH)

    def finish(ref, k):
        pltpu.make_async_copy(ref, ref, ssem.at[k]).wait()
        pltpu.make_async_copy(ref, ref, rsem.at[k]).wait()

    barrier = pltpu.get_barrier_semaphore()

    def greet(i, c):
        pl.semaphore_signal(barrier, inc=1, device_id={"seq": lax.bitwise_xor(me, i)}, device_id_type=MESH)
        return c

    lax.fori_loop(1, n, greet, 0, unroll=UNROLL)
    for i in range(8):
        pl.semaphore_signal(
            barrier, inc=1, device_id={"dp": 1 - core, "seq": lax.bitwise_xor(z, i) * 16 + xy}, device_id_type=MESH)

    loads[0].wait()
    loads[1].wait()
    for k in range(8):
        src = (sig_ref, cot_ref)[k // 4]
        block = src[:, (k % 4) * width:(k % 4 + 1) * width].astype(F32)
        stage[pl.ds(k, n, stride=8), :] = block.T
    send1[...] = stage[...].reshape(n, 8, width).astype(BF16)

    pl.semaphore_wait(barrier, n + 7)

    def post1(i, c):
        t = lax.bitwise_xor(me, i)
        remote(send1.at[t], recv1.at[me], 0, t).start()
        return c

    for q in FAR_FIRST:
        lax.fori_loop(max(16 * q, 1), 16 * q + 16, post1, 0, unroll=UNROLL)
    recv1[me] = send1[me]

    for load in loads[2:]:
        load.wait()
    lane = lax.broadcasted_iota(jnp.int32, (1, width), 1)
    wide = jnp.zeros((2 * modes, width), F32)
    slim = jnp.zeros((modes, width), F32)
    for j in range(4):
        for d in range(2):
            k = j * 2 + d
            cols = slice(j * width, (j + 1) * width)
            turn = lambda v, spot: pltpu.roll(v, lax.rem(spot + width - me, width), 1)
            wide = jnp.where(lane == k, turn(coef_ref[d, :, cols], k), wide)
            slim = jnp.where(lane == 8 + k, turn(rate_ref[d, :, cols], 8 + k), slim)
            slim = jnp.where(lane == 16 + k, turn(freq_ref[d, :, cols].astype(F32), 16 + k), slim)
    rows = jnp.where(lane < 8, wide, jnp.concatenate([slim, slim], axis=0)).T

    mat = lambda k: (mat_ref[k, 0], mat_ref[k, 1])
    outer, outer_t, inner, back = mat(0), mat(1), mat(2), mat(3)
    tcos, tsin = twist_ref[0], twist_ref[1]
    shift = jnp.where(lane < modes, 0.0, 0.75)
    spot = lax.broadcasted_iota(jnp.int32, (n, 1), 0).astype(F32)
    first = (lax.broadcasted_iota(jnp.int32, (n, width), 0) == 0) & (
        lax.broadcasted_iota(jnp.int32, (n, width), 1) == 0)
    scale = 2.0 * (modes * n * width) ** -0.5

    def twisted(a):
        re, im = a[:n], a[n:]
        return jnp.concatenate([re * tcos + im * tsin, im * tcos - re * tsin], axis=1)

    def untwist(b):
        re, im = b[:, :width], b[:, width:]
        return jnp.concatenate([re * tcos - im * tsin, im * tcos + re * tsin], axis=0)

    for j in range(4):
        halves = []
        for d in range(2):
            k = j * 2 + d
            raw, rate, freq = rows[k:k + 1], rows[8 + k:9 + k] * (1.0 / (n * width)), rows[16 + k:17 + k]
            swap = jnp.concatenate([raw[:, modes:], raw[:, :modes]], axis=1)
            c1 = jnp.where(lane < modes, raw, -swap) * scale
            c2 = jnp.where(lane < modes, -swap, -raw) * scale
            fa = fade_table(rate, freq, shift, spot if d == 0 else (n - 1.0) - spot, float(width), float(n))
            fb = fade_table(rate, freq, shift, spot if d == 0 else width - spot, 1.0, float(n * width))
            fades[k, 0] = fa
            fades[k, 1] = fb
            mixed = c1 * fa + c2 * pltpu.roll(fa, modes, 1)
            a, b = split(mixed), split(fb)
            nt = lambda x, y: lax.dot_general(x, y, (((1,), (1,)), ((), ())), preferred_element_type=F32)
            half = nt(a[0], b[0]) + nt(a[1], b[0]) + nt(a[0], b[1])
            halves.append(half if d == 0 else jnp.where(first, 0.0, half))
        wave = jnp.concatenate(halves, axis=0)
        kspec[j] = dot3(split(twisted(dot3(outer, split(wave)))), inner)

    finish(recv1.at[pl.ds(0, n - 1)], 0)
    stage[...] = recv1[...].astype(F32).reshape(8 * n, width)
    outer_cat = jnp.concatenate([outer[0][:, :n], outer[1][:, :n]], axis=1)

    def channel(i, skip_row):
        j = lax.rem(2 * (1 - core) + i, 4)
        s = stage[pl.ds(j, n, stride=8), :]
        g = stage[pl.ds(j + 4, n, stride=8), :]
        total = jnp.sum(jnp.sum(s * g, axis=0, keepdims=True), axis=1, keepdims=True)
        skip_row = skip_row + jnp.where(lane == j, total, 0.0)
        x = jnp.concatenate([s, g], axis=1).astype(BF16)
        a = dot(outer_cat, jnp.concatenate([x, x], axis=0))
        both = jnp.concatenate([twisted(a[:, :width]), twisted(a[:, width:])], axis=0)
        spec = dot3(split(both), inner)
        sre, sim, gre, gim = spec[:n, :width], spec[:n, width:], spec[n:, :width], spec[n:, width:]
        kre, kim = kspec[j, :, :width], kspec[j, :, width:]
        through[j, :, :width] = gre * kre + gim * kim
        through[j, :, width:] = gim * kre - gre * kim
        corr_out[i, :, :width] = gre * sre + gim * sim
        corr_out[i, :, width:] = gim * sre - gre * sim
        gain = jnp.sum(jnp.where(lane == me, gain_ref[pl.ds(j, 1), :], 0.0), axis=1, keepdims=True)
        direct[j] = gain * g
        return skip_row

    skip_row = jnp.zeros((1, width), F32)
    for i in range(2):
        skip_row = channel(i, skip_row)
    to_peer = remote(corr_out.at[pl.ds(0, 2)], corr_in, 1, None, True)
    to_peer.start()
    for i in range(2, 4):
        skip_row = channel(i, skip_row)

    to_peer.wait()
    corr = (corr_out[2:4] + corr_in[...]).reshape(2 * n, 2 * width)
    b = dot3(split(corr), back)
    cols = jnp.concatenate([untwist(b[:n]), untwist(b[n:])], axis=1)
    w = dot3(outer_t, split(cols))
    grads = []
    for jj in range(2):
        for d in range(2):
            k = (2 * core + jj) * 2 + d
            fa, fb = fades[k, 0], fades[k, 1]
            part = w[d * n:(d + 1) * n, jj * width:(jj + 1) * width]
            if d:
                part = jnp.where(first, 0.0, part)
            t = dot3(split(part), split(fb))
            p = jnp.sum(fa * t, axis=0, keepdims=True)
            q = jnp.sum(fa * pltpu.roll(t, modes, 1), axis=0, keepdims=True)
            p2 = jnp.concatenate([p[:, modes:], p[:, :modes]], axis=1)
            q2 = jnp.concatenate([q[:, modes:], q[:, :modes]], axis=1)
            grads.append(jnp.where(lane < modes, p - p2, -(q + q2)) * scale)
    skip_high = skip_row.astype(BF16).astype(F32)
    blank = jnp.zeros((2, width), F32)
    slot = core * 8 + z
    gmid[slot] = jnp.concatenate(grads + [skip_high, skip_row - skip_high, blank], axis=0).astype(BF16)

    for i in range(1, 8):
        for other in (False, True):
            remote(gmid.at[slot], gmid.at[slot], 2, lax.bitwise_xor(z, i) * 16 + xy, other).start()
    remote(gmid.at[slot], gmid.at[slot], 2, None, True).start()
    b = dot3(split(through[...].reshape(4 * n, 2 * width)), back)
    cols = jnp.concatenate([untwist(b[j * n:(j + 1) * n]) for j in range(4)], axis=1)
    y = dot3((outer_t[0][:n], outer_t[1][:n]), split(cols))
    for j in range(4):
        stage2[pl.ds(j, n, stride=4), :] = y[:, j * width:(j + 1) * width] + direct[j]
    send2[...] = stage2[:4 * n].reshape(n, 4, width).astype(BF16)

    def post2(i, c):
        t = lax.bitwise_xor(me, i)
        remote(send2.at[t], recv2.at[me], 4, t).start()
        return c

    for q in FAR_FIRST[:8]:
        lax.fori_loop(max(16 * q, 1), 16 * q + 16, post2, 0, unroll=UNROLL)
    finish(gmid.at[pl.ds(0, 15)], 2)
    seen = gmid[...].astype(F32)
    gsend[pl.ds(0, 16)] = seen[:, :4].astype(BF16)
    skips = jnp.zeros((2, width), F32)
    for q in range(8):
        part = seen[q, 4:5] + seen[q, 5:6] + (seen[8 + q, 4:5] + seen[8 + q, 5:6])
        part = pltpu.roll(part, 4 * q, 1) if q else part
        high = part.astype(BF16).astype(F32)
        skips = skips + jnp.concatenate([high, part - high], axis=0)
    gsend[16] = jnp.concatenate([skips, blank], axis=0).astype(BF16)
    for i in range(1, 16):
        remote(gsend, gall.at[xy], 3, z * 16 + lax.bitwise_xor(xy, i)).start()
    for q in FAR_FIRST[8:]:
        lax.fori_loop(max(16 * q, 1), 16 * q + 16, post2, 0, unroll=UNROLL)
    recv2[me] = send2[me]
    gall[xy] = gsend[...]

    finish(recv2.at[pl.ds(0, n - 1)], 4)
    stage[:4 * n] = recv2[...].astype(F32).reshape(4 * n, width)
    for j in range(4):
        out_ref[:, j * width:(j + 1) * width] = stage[pl.ds(j, n, stride=4), :].T.astype(BF16)
    finish(gall.at[pl.ds(0, 15)], 3)
    stage2[...] = gall[...].astype(F32).reshape(17 * 64, width)
    skips = (stage2[pl.ds(64, 16, stride=68), :] + stage2[pl.ds(65, 16, stride=68), :]).T
    gskip_ref[...] = jnp.concatenate([skips[4 * q:4 * q + 4] for q in range(8)], axis=1)
    for c in range(2):
        for jj in range(2):
            for d in range(2):
                block = jnp.concatenate([
                    stage2[pl.ds((8 * c + q) * 4 + jj * 2 + d, 16, stride=68), :] for q in range(8)], axis=0).T
                cols = slice((2 * c + jj) * width, (2 * c + jj + 1) * width)
                gcoef_ref[d, :, cols] = block.astype(BF16)


def finals(out_in, gcoef_in, gskip_in, out, gcoef, gskip, low, wide, y, sem):
    copy = lambda src, dst, k: pltpu.make_async_copy(src, dst, sem.at[k])
    rows = low.shape[1] // 2
    parts = [(d, pl.ds(h * rows, rows)) for d in range(2) for h in range(2)]
    loads = [copy(gcoef_in.at[p], low.at[p], k) for k, p in enumerate(parts)]
    moves = [copy(gskip_in, gskip, 9)]
    load_y = copy(out_in, y, 8)
    for move in [load_y] + loads + moves:
        move.start()
    load_y.wait()
    moves.append(copy(y, out, 10))
    moves[-1].start()
    for k, p in enumerate(parts):
        loads[k].wait()
        wide[p] = low[p].astype(F32)
        moves.append(copy(wide.at[p], gcoef.at[p], 4 + k))
        moves[-1].start()
    for move in moves:
        move.wait()


def on_device(signal, grad_out, mode_coef, decay_param, freq_index, skip_gain):
    n = lax.axis_size("seq")
    width, channels = signal.shape[1:]
    modes = decay_param.shape[1]
    mats, twist = tables(n, width)
    vmem = pl.BlockSpec(memory_space=pltpu.VMEM)
    operands = (signal[0], grad_out[0], mode_coef.reshape(2, 2 * modes, channels), decay_param, freq_index,
                skip_gain.reshape(channels // width, width), mats, twist)
    out = pl.pallas_call(
        functools.partial(kernel, n, modes),
        out_shape=(
            jax.ShapeDtypeStruct((width, channels), BF16),
            jax.ShapeDtypeStruct((2, 2 * modes, channels), BF16),
            jax.ShapeDtypeStruct((channels // width, n), F32),
        ),
        in_specs=[pl.BlockSpec(memory_space=pl.ANY)] * 8,
        out_specs=(vmem,) * 3,
        scratch_shapes=[pltpu.VMEM(t.shape, t.dtype) for t in operands] + [
            pltpu.SemaphoreType.DMA((8,)),
            pltpu.VMEM((8 * n, width), F32),
            pltpu.VMEM((17 * 64, width), F32),
            pltpu.VMEM((n, 8, width), BF16),
            pltpu.VMEM((n, 8, width), BF16),
            pltpu.VMEM((n, 4, width), BF16),
            pltpu.VMEM((n, 4, width), BF16),
            pltpu.VMEM((4, n, 2 * width), F32),
            pltpu.VMEM((4, n, 2 * width), F32),
            pltpu.VMEM((4, n, 2 * width), F32),
            pltpu.VMEM((2, n, 2 * width), F32),
            pltpu.VMEM((8, 2, n, 2 * modes), F32),
            pltpu.VMEM((4, n, width), F32),
            pltpu.VMEM((16, 8, width), BF16),
            pltpu.VMEM((17, 4, width), BF16),
            pltpu.VMEM((16, 17, 4, width), BF16),
            pltpu.SemaphoreType.DMA((8,)),
            pltpu.SemaphoreType.DMA((8,)),
        ],
        compiler_params=pltpu.CompilerParams(
            collective_id=0, has_side_effects=True, vmem_limit_bytes=ROOM),
    )(*operands)
    hbm = pl.BlockSpec(memory_space=pl.ANY)
    out = pl.pallas_call(
        finals,
        out_shape=tuple(jax.ShapeDtypeStruct(t.shape, d) for t, d in zip(out, (BF16, F32, F32))),
        in_specs=[hbm] * 3,
        out_specs=(hbm,) * 3,
        scratch_shapes=[
            pltpu.VMEM(out[1].shape, BF16),
            pltpu.VMEM(out[1].shape, F32),
            pltpu.VMEM(out[0].shape, BF16),
            pltpu.SemaphoreType.DMA((11,)),
        ],
        compiler_params=pltpu.CompilerParams(vmem_limit_bytes=ROOM),
    )(*out)
    return (out[0][None], out[1].reshape(mode_coef.shape), out[2].reshape(channels))


def solution(mesh):
    return jax.shard_map(
        on_device,
        mesh=mesh,
        in_specs=(P("dp", "seq", None), P("dp", "seq", None), P(), P(), P(), P()),
        out_specs=(P("dp", "seq", None), P(), P()),
        check_vma=False,
    )
```
